256 devices in a mesh: dp: 32 (over z_lo, x, core), mp: 8 (over z_hi, y).
Axes of the slice: x: 4, y: 4, z: 8 (z_hi: 2, z_lo: 4; z = z_hi * 4 + z_lo), core: 2. Of those that a mesh axis runs over, the one named last changes fastest.
Arguments:
- tokens: bfloat16 [16384, 128, 128], P('dp', 'mp'), may hold values from -6 to 6
- left_factor: float32 [128, 128, 128], P('mp', 'dp'), may hold values from -0.5 to 0.5
- right_factor: float32 [128, 128, 128], P('mp', 'dp'), may hold values from -0.5 to 0.5
- target: bfloat16 [16384, 128, 128], P('dp', 'mp'), may hold values from -6 to 6
Outputs:
- token_grad: bfloat16 [16384, 128, 128], P('dp', 'mp')
- left_grad: float32 [128, 128, 128], P('mp', 'dp')
- right_grad: float32 [128, 128, 128], P('mp', 'dp')
The draws below stay inside these ranges and needn't reach their ends.
All inputs are finite; a program needn't handle non-finite values.
Results may differ from the reference program's by a relative error of at most 0.024.
Values may be sent and summed in bfloat16 or wider, within the bound.
A program may use at most 64 MiB of HBM per device.

```python
import jax
import jax.numpy as jnp
from jax import lax

BLOCKS = 128
BSIZE = 128
TOK_DEV = 512
TOKENS = 16384
N_DP = 32


def block_levels(key, extent, cuts, least, top_value):
    def one(dim, shards_of):
        steps = jax.random.uniform(jax.random.fold_in(jax.random.fold_in(key, 6), dim), (shards_of,), jnp.float32, least / len(cuts), top_value / len(cuts))
        return jnp.repeat(jnp.exp(steps), extent[dim] // shards_of).reshape((-1,) + (1,) * (len(extent) - dim - 1))

    gain = one(*cuts[0])
    for cut in cuts[1:]:
        gain = gain * one(*cut)
    return gain


def bell_draw(own_key, extent, spread, reach, shards=(), dtype=jnp.bfloat16):
    result = jax.random.normal(own_key, extent, jnp.float32) * spread
    if len(shards) > 0:
        result = block_levels(own_key, extent, shards, -0.22, 0.18) * result
    return jnp.clip(result, min=-reach, max=reach).astype(dtype)


def setup_inputs(seed: int = 0) -> dict:
    seeds = jax.random.split(jax.random.key(seed), 5)
    return {
        "tokens": bell_draw(seeds[0], (TOKENS, BLOCKS, BSIZE), 1.0, 6.0, ((0, 32), (1, 8))),
        "left_factor": bell_draw(seeds[1], (BLOCKS, BSIZE, BSIZE), BSIZE ** -0.5, 0.5, ((0, 8), (1, 32)), jnp.float32),
        "right_factor": bell_draw(seeds[2], (BSIZE, BLOCKS, BSIZE), BLOCKS ** -0.5, 0.5, ((0, 8), (1, 32)), jnp.float32),
        "target": bell_draw(seeds[3], (TOKENS, BSIZE, BSIZE), 1.0, 6.0, ((0, 32), (1, 8))),
    }


def to_bf(value):
    return lax.optimization_barrier(value.astype(jnp.bfloat16)).astype(jnp.float32)

def reference(tokens, left_factor, right_factor, target):
    left_f = to_bf(left_factor)
    right_f = to_bf(right_factor)
    x_blocks = tokens.reshape(N_DP, TOK_DEV, BLOCKS, BSIZE)
    t_blocks = target.reshape(N_DP, TOK_DEV, BSIZE, BSIZE)

    def advance(carry, item):
        left_acc, right_acc = carry
        x_part, t_part = item
        x_float = x_part.astype(jnp.float32)
        pre = jnp.einsum('tbi,bij->tbj', x_float, left_f)
        act = to_bf(jax.nn.gelu(pre))
        perm = jnp.swapaxes(act, 1, 2)
        out = jnp.einsum('tjb,jbk->tjk', perm, right_f)
        dout = to_bf(out - t_part.astype(jnp.float32))
        right_acc = right_acc + jnp.einsum('tjb,tjk->jbk', perm, dout)
        dperm = to_bf(jnp.einsum('tjk,jbk->tjb', dout, right_f))
        dact = jnp.swapaxes(dperm, 1, 2)
        pull = jax.vjp(jax.nn.gelu, pre)[1]
        dpre = to_bf(pull(dact)[0])
        left_acc = left_acc + jnp.einsum('tbi,tbj->bij', x_float, dpre)
        grad_x = jnp.einsum('tbj,bij->tbi', dpre, left_f).astype(jnp.bfloat16)
        return ((left_acc, right_acc), grad_x)
    start = (jnp.zeros((BLOCKS, BSIZE, BSIZE), jnp.float32), jnp.zeros((BSIZE, BLOCKS, BSIZE), jnp.float32))
    (left_grad, right_grad), grads = lax.scan(advance, start, (x_blocks, t_blocks))
    token_grad = grads.reshape(TOKENS, BLOCKS, BSIZE)
    return (token_grad, left_grad, right_grad)
```

```python
import functools

import jax
import jax.numpy as jnp
from jax import lax
from jax.experimental import pallas as pl
from jax.experimental.pallas import tpu as pltpu
from jax.sharding import PartitionSpec as P

MESH = pl.DeviceIdType.MESH
BF, F32 = jnp.bfloat16, jnp.float32
CH = 4
TC = 128
GELU_K = 0.7978845608028654
GELU_C = 0.044715


def mm(a, b):
    return jnp.dot(a, b, preferred_element_type=F32)


def mm_nt(a, b):
    return lax.dot_general(a, b, (((1,), (1,)), ((), ())), preferred_element_type=F32)


def loop(n, body, unroll=1):
    def step(i, carry):
        body(i)
        return carry

    lax.fori_loop(0, n, step, 0, unroll=unroll)


def low_half():
    return lax.broadcasted_iota(jnp.int32, (8, 8, 128), 1) < 4


def kernel(
    tok_hbm, wl_ref, wr_ref, tgt_hbm,
    tg_hbm, lg_out, rg_out,
    tok_raw, tgt_raw, tokT, tgtT, stage, stage2,
    gath, wfull, lw, lwT, rw, rwT,
    gp, fsend, frecv, bsend, brecv, lgrad, rgrad, tgbuf,
    rs0, rs_c, rs1, rs_x, rs2, rs_z,
    in_sem, out_sem, agz_s, agz_r, agx_s, agx_r, agc_s, agc_r,
    f_s, f_r, b_s, b_r, rc_s, rc_r, rx_s, rx_r, rz_s, rz_r,
):
    dp, mp = lax.axis_index("dp"), lax.axis_index("mp")
    z, x, core = dp // 8, lax.rem(dp // 2, 4), lax.rem(dp, 2)

    def z_peer(o):
        return (lax.rem(z + o, 4) * 8 + x * 2 + core, mp)

    def x_peer(o):
        return (z * 8 + lax.rem(x + o, 4) * 2 + core, mp)

    c_peer = (z * 8 + x * 2 + (1 - core), mp)

    def m_peer(o):
        return (dp, lax.rem(mp + o, 8))

    def remote(src, dst, ss, rs, dev):
        return pltpu.make_async_remote_copy(
            src_ref=src, dst_ref=dst, send_sem=ss, recv_sem=rs, device_id=dev, device_id_type=MESH
        )

    def tok_in(c):
        return pltpu.make_async_copy(tok_hbm.at[pl.ds(c * TC, TC)], tok_raw.at[c], in_sem.at[0, c])

    def tgt_in(c):
        return pltpu.make_async_copy(tgt_hbm.at[pl.ds(c * TC, TC)], tgt_raw.at[c], in_sem.at[1, c])

    loop(CH, lambda c: tok_in(c).start())
    loop(CH, lambda c: tgt_in(c).start())

    barrier = pltpu.get_barrier_semaphore()
    peers = [z_peer(o) for o in (1, 2, 3)] + [x_peer(o) for o in (1, 2, 3)] + [c_peer]
    peers += [m_peer(o) for o in range(1, 8)]
    for dev in peers:
        pl.semaphore_signal(barrier, inc=1, device_id=dev, device_id_type=MESH)
    gath[0, core, x, z] = wl_ref[...].astype(BF)
    gath[1, core, x, z] = wr_ref[...].astype(BF)
    pl.semaphore_wait(barrier, len(peers))

    def ag_z(f, o):
        piece = gath.at[f, core, x, z]
        return remote(piece, piece, agz_s.at[f, o - 1], agz_r.at[f, o - 1], z_peer(o))

    def ag_x(f, o):
        piece = gath.at[f, core, x]
        return remote(piece, piece, agx_s.at[f, o - 1], agx_r.at[f, o - 1], x_peer(o))

    def ag_c(f, o):
        piece = gath.at[f, core, lax.rem(x + 4 - o, 4)]
        return remote(piece, piece, agc_s.at[f, o], agc_r.at[f, o], c_peer)

    for f in (0, 1):
        for o in (1, 2, 3):
            ag_z(f, o).start()

    def spread(raw, outT, c):
        stage[...] = raw[c].astype(F32).reshape(TC * 16, 128)

        def one(n):
            rows = stage[pl.ds(n, TC, stride=16), :]
            outT[c, n] = rows.T.astype(BF)

        loop(16, one, 4)

    tok_in(0).wait()
    spread(tok_raw, tokT, 0)
    for f in (0, 1):
        for o in (1, 2, 3):
            ag_z(f, o).wait_recv()
        for o in (1, 2, 3):
            ag_x(f, o).start()
        ag_c(f, 0).start()

    def assemble(f, w, wT):
        def pair(m):
            mx, mz = lax.rem(m, 4), m // 4
            a = gath[f, 0, mx, mz].astype(F32).reshape(8, 8, 128)
            b = gath[f, 1, mx, mz].astype(F32).reshape(8, 8, 128)
            low = low_half()
            rows = pl.ds(pl.multiple_of(m * 8, 8), 8)
            wfull[:, 0, rows, :] = jnp.where(low, a, pltpu.roll(b, 4, 1))
            wfull[:, 1, rows, :] = jnp.where(low, pltpu.roll(a, 4, 1), b)

        loop(16, pair, 2)

        def one(n):
            full = wfull[n // 2, lax.rem(n, 2)]
            w[n] = full.astype(BF)
            wT[n] = full.T.astype(BF)

        loop(16, one, 2)

    def finish_gather(f):
        for o in (1, 2, 3):
            ag_x(f, o).wait_recv()
            ag_c(f, o).start()
        for o in (0, 1, 2, 3):
            ag_c(f, o).wait_recv()

    finish_gather(0)
    assemble(0, lw, lwT)

    def fwd_copy(c, o):
        return remote(
            fsend.at[c, lax.rem(mp + o, 8)], frecv.at[c, mp], f_s.at[c, o - 1], f_r.at[c, o - 1], m_peer(o)
        )

    def bwd_copy(c, o):
        return remote(
            bsend.at[c, lax.rem(mp + o, 8)], brecv.at[c, mp], b_s.at[c, o - 1], b_r.at[c, o - 1], m_peer(o)
        )

    def regroup(src, g, dst):
        for m in range(16):
            dst(m, src[pl.ds(g * 16 + m, 16, stride=128), :].astype(BF))

    def forward(c):
        def one(n):
            pre = mm(lwT[n], tokT[c, n])
            sq = pre * pre
            th = jnp.tanh(pre * (GELU_K + (GELU_K * GELU_C) * sq))
            half = 0.5 + 0.5 * th
            gp[c, n] = half + (0.5 * pre) * (1.0 - th * th) * (GELU_K + (3.0 * GELU_K * GELU_C) * sq)
            stage2[pl.ds(pl.multiple_of(n * 128, 128), 128), :] = pre * half

        loop(16, one, 2)

        def send(i):
            o = i + 1
            g = lax.rem(mp + o, 8)

            def put(m, v):
                fsend[c, g, m] = v

            regroup(stage2, g, put)
            fwd_copy(c, o).start()

        loop(7, send)

        def keep(m, v):
            frecv[c, mp, m] = v

        regroup(stage2, mp, keep)

    forward(0)

    def more(i):
        c = i + 1
        tok_in(c).wait()
        spread(tok_raw, tokT, c)
        forward(c)

    loop(CH - 1, more)

    finish_gather(1)
    assemble(1, rw, rwT)

    def targets(c):
        tgt_in(c).wait()
        spread(tgt_raw, tgtT, c)

    loop(CH, targets)

    lgrad[...] = jnp.zeros_like(lgrad)
    rgrad[...] = jnp.zeros_like(rgrad)

    def right(c):
        loop(7, lambda i: fwd_copy(c, i + 1).wait_recv())

        def one(n):
            act = frecv[c, :, n].reshape(128, TC)
            out = mm(rwT[n], act)
            dout = (out - tgtT[c, n].astype(F32)).astype(BF)
            q, s = n // 2, lax.rem(n, 2)
            rgrad[q, s] = rgrad[q, s] + mm_nt(act, dout)
            stage2[pl.ds(pl.multiple_of(n * 128, 128), 128), :] = mm(rw[n], dout)

        loop(16, one, 2)

        def send(i):
            o = i + 1
            g = lax.rem(mp + o, 8)

            def put(m, v):
                bsend[c, g, m] = v

            regroup(stage2, g, put)
            bwd_copy(c, o).start()

        loop(7, send)

        def keep(m, v):
            brecv[c, mp, m] = v

        regroup(stage2, mp, keep)

    loop(CH, right)

    def pieces(f, grad):
        def pair(m):
            mx, mz = lax.rem(m, 4), m // 4
            rows = pl.ds(pl.multiple_of(m * 8, 8), 8)
            a, b = grad[:, 0, rows, :], grad[:, 1, rows, :]
            low = low_half()
            rs0[f, 0, mx, mz] = jnp.where(low, a, pltpu.roll(b, 4, 1)).reshape(64, 128).astype(BF)
            rs0[f, 1, mx, mz] = jnp.where(low, pltpu.roll(a, 4, 1), b).reshape(64, 128).astype(BF)

        loop(16, pair, 2)

    def rs_core(f):
        return remote(rs0.at[f, 1 - core], rs_c.at[f], rc_s.at[f], rc_r.at[f], c_peer)

    def rs_xx(f, o):
        return remote(
            rs1.at[f, lax.rem(x + o, 4)], rs_x.at[f, o - 1], rx_s.at[f, o - 1], rx_r.at[f, o - 1], x_peer(o)
        )

    def rs_zz(f, o):
        return remote(
            rs2.at[f, lax.rem(z + o, 4)], rs_z.at[f, o - 1], rz_s.at[f, o - 1], rz_r.at[f, o - 1], z_peer(o)
        )

    def rs_start(f, grad):
        pieces(f, grad)
        rs_core(f).start()

    def rs_second(f):
        rs_core(f).wait_recv()

        def add(m):
            mx, mz = m // 4, lax.rem(m, 4)
            rs1[f, mx, mz] = (rs0[f, core, mx, mz].astype(F32) + rs_c[f, mx, mz].astype(F32)).astype(BF)

        loop(16, add, 2)
        for o in (1, 2, 3):
            rs_xx(f, o).start()

    def rs_third(f):
        for o in (1, 2, 3):
            rs_xx(f, o).wait_recv()

        def add(m):
            total = rs1[f, x, m].astype(F32)
            for o in range(3):
                total = total + rs_x[f, o, m].astype(F32)
            rs2[f, m] = total.astype(BF)

        loop(4, add)
        for o in (1, 2, 3):
            rs_zz(f, o).start()

    def rs_last(f, out):
        for o in (1, 2, 3):
            rs_zz(f, o).wait_recv()
        total = rs2[f, z].astype(F32)
        for o in range(3):
            total = total + rs_z[f, o].astype(F32)
        out[...] = total

    def tg_out(c):
        rows = pl.ds(pl.multiple_of(c * TC, TC), TC)
        return pltpu.make_async_copy(tgbuf.at[:, rows, :], tg_hbm.at[:, rows, :], out_sem.at[c])

    def left(c):
        loop(7, lambda i: bwd_copy(c, i + 1).wait_recv())

        def one(n):
            back = brecv[c, :, n].reshape(128, TC).astype(F32)
            dpre = (back * gp[c, n]).astype(BF)
            q, s = n // 2, lax.rem(n, 2)
            lgrad[q, s] = lgrad[q, s] + mm_nt(tokT[c, n], dpre)
            grad = mm(lw[n], dpre)
            tgbuf[n, pl.ds(pl.multiple_of(c * TC, TC), TC), :] = grad.T.astype(BF)

        loop(16, one, 2)
        tg_out(c).start()

    rs_start(1, rgrad)
    left(0)
    rs_second(1)
    left(1)
    rs_third(1)
    left(2)
    rs_last(1, rg_out)
    left(3)
    rs_start(0, lgrad)
    rs_second(0)
    rs_third(0)
    rs_last(0, lg_out)

    for f in (0, 1):
        for o in (1, 2, 3):
            ag_z(f, o).wait_send()
            ag_x(f, o).wait_send()
            rs_xx(f, o).wait_send()
            rs_zz(f, o).wait_send()
        for o in (0, 1, 2, 3):
            ag_c(f, o).wait_send()
        rs_core(f).wait_send()

    def drain(c):
        loop(7, lambda i: fwd_copy(c, i + 1).wait_send())
        loop(7, lambda i: bwd_copy(c, i + 1).wait_send())
        tg_out(c).wait()

    loop(CH, drain)


def step(tokens, left_factor, right_factor, target):
    V = pltpu.VMEM
    D = pltpu.SemaphoreType.DMA
    any_spec = pl.BlockSpec(memory_space=pl.ANY)
    vmem_spec = pl.BlockSpec(memory_space=pltpu.VMEM)
    sq = (128, 128)
    scratch = [
        V((CH, TC, 16, 128), BF), V((CH, TC, 16, 128), BF),
        V((CH, 16, 128, TC), BF), V((CH, 16, 128, TC), BF),
        V((TC * 16, 128), F32), V((16 * 128, TC), F32),
        V((2, 2, 4, 4, 64, 128), BF), V((8, 2) + sq, F32),
        V((16,) + sq, BF), V((16,) + sq, BF), V((16,) + sq, BF), V((16,) + sq, BF),
        V((CH, 16, 128, TC), F32),
        V((CH, 8, 16, 16, TC), BF), V((CH, 8, 16, 16, TC), BF),
        V((CH, 8, 16, 16, TC), BF), V((CH, 8, 16, 16, TC), BF),
        V((8, 2) + sq, F32), V((8, 2) + sq, F32),
        V((16, CH * TC, 128), BF),
        V((2, 2, 4, 4, 64, 128), BF), V((2, 4, 4, 64, 128), BF),
        V((2, 4, 4, 64, 128), BF), V((2, 3, 4, 64, 128), BF),
        V((2, 4, 64, 128), BF), V((2, 3, 64, 128), BF),
        D((2, CH)), D((CH,)),
        D((2, 3)), D((2, 3)), D((2, 3)), D((2, 3)), D((2, 4)), D((2, 4)),
        D((CH, 7)), D((CH, 7)), D((CH, 7)), D((CH, 7)),
        D((2,)), D((2,)), D((2, 3)), D((2, 3)), D((2, 3)), D((2, 3)),
    ]
    tg, lg, rg = pl.pallas_call(
        kernel,
        name="monarch",
        out_shape=(
            jax.ShapeDtypeStruct((16, CH * TC, 128), BF),
            jax.ShapeDtypeStruct((64, 128), F32),
            jax.ShapeDtypeStruct((64, 128), F32),
        ),
        in_specs=[any_spec, vmem_spec, vmem_spec, any_spec],
        out_specs=(any_spec, vmem_spec, vmem_spec),
        scratch_shapes=scratch,
        compiler_params=pltpu.CompilerParams(
            collective_id=0, has_side_effects=True, vmem_limit_bytes=48 << 20
        ),
    )(tokens, left_factor.reshape(64, 128), right_factor.reshape(64, 128), target)
    return tg.transpose(1, 0, 2), lg.reshape(16, 4, 128), rg.reshape(16, 4, 128)


def solution(mesh):
    in_specs = (P("dp", "mp", None), P("mp", "dp", None), P("mp", "dp", None), P("dp", "mp", None))
    out_specs = (P("dp", "mp", None), P("mp", "dp", None), P("mp", "dp", None))
    return jax.shard_map(step, mesh=mesh, in_specs=in_specs, out_specs=out_specs, check_vma=False)
```

```python
import jax
import jax.numpy as jnp
from jax import lax
from jax.experimental import pallas as pl
from jax.experimental.pallas import tpu as pltpu
from jax.sharding import PartitionSpec as P

MESH = pl.DeviceIdType.MESH
BF, F32 = jnp.bfloat16, jnp.float32
CH = 4
TC = 128
LAST = CH - 1
GELU_K = 0.7978845608028654
GELU_C = 0.044715


def mm(a, b):
    return jnp.dot(a, b, preferred_element_type=F32)


def mm_nt(a, b):
    return lax.dot_general(a, b, (((1,), (1,)), ((), ())), preferred_element_type=F32)


def loop(lo, hi, body, unroll=1):
    def step(i, carry):
        body(i)
        return carry

    lax.fori_loop(lo, hi, step, 0, unroll=unroll)


def aligned(i, size):
    return pl.ds(pl.multiple_of(i * size, size), size)


def low_half():
    return lax.broadcasted_iota(jnp.int32, (1, 8, 128), 1) < 4


def kernel(
    tok_hbm, wl_hbm, wr_hbm, tgt_hbm,
    tg_out, lg_out, rg_out,
    tok_raw, tgt_raw, w_raw, tokT, tgtT, stage, stage2, stage3,
    gath, wfull, lw, lwT, rw, rwT,
    gp, fsend, frecv, bsend, brecv, lgrad, rgrad,
    rs0, rs_x, rs2, rs_z,
    in_sem, w_sem, agz_s, agz_r, agx_s, agx_r, agc_s, agc_r,
    f_s, f_r, b_s, b_r, q_s, q_r, rx_s, rx_r, rz_s, rz_r, qx_s, qx_r, qz_s, qz_r,
):
    dp, mp = lax.axis_index("dp"), lax.axis_index("mp")
    z, x, core = dp // 8, lax.rem(dp // 2, 4), lax.rem(dp, 2)
    hi, y = mp // 4, lax.rem(mp, 4)

    def z_peer(o):
        return (lax.rem(z + o, 4) * 8 + x * 2 + core, mp)

    def xc_of(k):
        return lax.rem(x + lax.rem(k, 4), 4), lax.rem(core + k // 4, 2)

    def xc_peer(k):
        px, pc = xc_of(k)
        return (z * 8 + px * 2 + pc, mp)

    def m_of(k):
        return lax.rem(hi + k // 4, 2) * 4 + lax.rem(y + lax.rem(k, 4), 4)

    def remote(src, dst, ss, rs, dev):
        return pltpu.make_async_remote_copy(
            src_ref=src, dst_ref=dst, send_sem=ss, recv_sem=rs, device_id=dev, device_id_type=MESH
        )

    barrier = pltpu.get_barrier_semaphore()
    peers = [z_peer(o) for o in (1, 2, 3)] + [xc_peer(k) for k in range(1, 8)]
    peers += [(dp, m_of(k)) for k in range(1, 8)]
    for dev in peers:
        pl.semaphore_signal(barrier, inc=1, device_id=dev, device_id_type=MESH)

    def w_in(f):
        return pltpu.make_async_copy((wl_hbm, wr_hbm)[f], w_raw.at[f], w_sem.at[f])

    def tok_in(c):
        return pltpu.make_async_copy(tok_hbm.at[aligned(c, TC)], tok_raw.at[c], in_sem.at[0, c])

    def tgt_in(c):
        return pltpu.make_async_copy(tgt_hbm.at[aligned(c, TC)], tgt_raw.at[c], in_sem.at[1, c])

    for f in (0, 1):
        w_in(f).start()
    loop(0, CH, lambda c: tok_in(c).start())
    loop(0, CH, lambda c: tgt_in(c).start())
    for f in (0, 1):
        w_in(f).wait()
        for h in (0, 1):
            gath[f, h, core, x, z] = w_raw[f, 32 * h : 32 * h + 32].astype(BF)
    pl.semaphore_wait(barrier, len(peers))

    def ag_z(f, h, o):
        piece = gath.at[f, h, core, x, z]
        return remote(piece, piece, agz_s.at[f, h, o - 1], agz_r.at[f, h, o - 1], z_peer(o))

    def ag_x(f, h, o):
        piece = gath.at[f, h, core, x]
        return remote(piece, piece, agx_s.at[f, h, o - 1], agx_r.at[f, h, o - 1], xc_peer(o))

    def ag_c(f, h, o):
        piece = gath.at[f, h, core, lax.rem(x + 4 - o, 4)]
        return remote(piece, piece, agc_s.at[f, h, o], agc_r.at[f, h, o], xc_peer(4))

    def gather_first(f, h):
        for o in (1, 2, 3):
            ag_z(f, h, o).start()

    def gather_second(f, h):
        for o in (1, 2, 3):
            ag_z(f, h, o).wait_recv()
        for o in (1, 2, 3):
            ag_x(f, h, o).start()
        ag_c(f, h, 0).start()

    def gather_third(f, h):
        for o in (1, 2, 3):
            ag_x(f, h, o).wait_recv()
            ag_c(f, h, o).start()

    def gather_end(f, h):
        for o in (0, 1, 2, 3):
            ag_c(f, h, o).wait_recv()

    def spread(raw, outT, c):
        stage[...] = raw[c].astype(F32).reshape(TC * 16, 128)

        def one(n):
            rows = stage[pl.ds(n, TC, stride=16), :]
            outT[c, n] = rows.T.astype(BF)

        loop(0, 16, one, 4)

    def tokens_ready(c):
        tok_in(c).wait()
        spread(tok_raw, tokT, c)

    def targets_ready(c):
        tgt_in(c).wait()
        spread(tgt_raw, tgtT, c)

    def assemble(f, h, w, wT):
        def pair(m):
            mx, mz = lax.rem(m, 4), m // 4
            a = gath[f, h, 0, mx, mz].astype(F32).reshape(4, 8, 128)
            b = gath[f, h, 1, mx, mz].astype(F32).reshape(4, 8, 128)
            low = low_half()
            rows = aligned(m, 8)
            wfull[4 * h : 4 * h + 4, 0, rows, :] = jnp.where(low, a, pltpu.roll(b, 4, 1))
            wfull[4 * h : 4 * h + 4, 1, rows, :] = jnp.where(low, pltpu.roll(a, 4, 1), b)

        loop(0, 16, pair, 4)

        def one(n):
            full = wfull[n // 2, lax.rem(n, 2)]
            w[n] = full.astype(BF)
            wT[n] = full.T.astype(BF)

        loop(8 * h, 8 * h + 8, one, 4)

    def fwd_copy(c, k):
        return remote(
            fsend.at[c, m_of(k)], frecv.at[c, mp], f_s.at[c, k - 1], f_r.at[c, k - 1], (dp, m_of(k))
        )

    def bwd_copy(c, k):
        return remote(
            bsend.at[c, m_of(k)], brecv.at[c, mp], b_s.at[c, k - 1], b_r.at[c, k - 1], (dp, m_of(k))
        )

    def quarter_copy(q, k):
        part = pl.ds(4 * q, 4)
        return remote(
            bsend.at[LAST, m_of(k), part], brecv.at[LAST, mp, part],
            q_s.at[q, k - 1], q_r.at[q, k - 1], (dp, m_of(k)),
        )

    def regroup(src, g, m):
        return src[pl.ds(g * 16 + m, 16, stride=128), :].astype(BF)

    def forward_part(c, jh, lo, hi_n):
        rows = aligned(jh, 64)

        def one(n):
            pre = mm(lwT[n, rows, :], tokT[c, n])
            sq = pre * pre
            th = jnp.tanh(pre * (GELU_K + (GELU_K * GELU_C) * sq))
            half = 0.5 + 0.5 * th
            gp[c, n, rows, :] = half + (0.5 * pre) * (1.0 - th * th) * (
                GELU_K + (3.0 * GELU_K * GELU_C) * sq
            )
            stage2[pl.ds(pl.multiple_of(n * 128 + jh * 64, 64), 64), :] = pre * half

        loop(lo, hi_n, one, 4)

    def forward_send(c, lo, hi_k):
        def send(k):
            g = m_of(k)
            for m in range(16):
                fsend[c, g, m] = regroup(stage2, g, m)
            fwd_copy(c, k).start()

        loop(lo, hi_k, send)

    def forward_rest(c):
        forward_part(c, hi, 0, 16)
        forward_send(c, 1, 4)
        for m in range(16):
            frecv[c, mp, m] = regroup(stage2, mp, m)

    for h in (0, 1):
        gather_first(0, h)
    tokens_ready(0)
    for h in (0, 1):
        gather_second(0, h)
    for h in (0, 1):
        gather_first(1, h)
    tokens_ready(1)
    for h in (0, 1):
        gather_third(0, h)
    for h in (0, 1):
        gather_second(1, h)
    for h in (0, 1):
        gather_end(0, h)
        assemble(0, h, lw, lwT)
        forward_part(0, 1 - hi, 8 * h, 8 * h + 8)
    forward_send(0, 4, 8)
    forward_rest(0)

    def forward(c):
        forward_part(c, 1 - hi, 0, 16)
        forward_send(c, 4, 8)
        forward_rest(c)

    forward(1)
    for h in (0, 1):
        gather_third(1, h)

    for h in (0, 1):
        gather_end(1, h)
        assemble(1, h, rw, rwT)

    lgrad[...] = jnp.zeros_like(lgrad)
    rgrad[...] = jnp.zeros_like(rgrad)

    def right(c):
        def one(n):
            act = frecv[c, :, n].reshape(128, TC)
            out = mm(rwT[n], act)
            dout = (out - tgtT[c, n].astype(F32)).astype(BF)
            q, s = n // 2, lax.rem(n, 2)
            rgrad[q, s] = rgrad[q, s] + mm_nt(act, dout)
            stage2[aligned(n, 128), :] = mm(rw[n], dout)

        loop(0, 16, one, 4)
        for m in range(16):
            brecv[c, mp, m] = regroup(stage2, mp, m)

        def fill(k):
            g = m_of(k)
            for m in range(16):
                bsend[c, g, m] = regroup(stage2, g, m)

        loop(1, 8, fill)

    def first(i):
        return lax.rem(i + 3, 7) + 1

    def send_back(c):
        loop(0, 7, lambda i: bwd_copy(c, first(i)).start())

    def turn(c):
        targets_ready(c)
        loop(1, 8, lambda k: fwd_copy(c, k).wait_recv())

        @pl.when(c < 2)
        def _():
            tokens_ready(c + 2)
            forward(c + 2)

        @pl.when(c == 2)
        def _():
            send_back(1)

        right(c)

        @pl.when(c == 0)
        def _():
            send_back(0)

        @pl.when(c == 2)
        def _():
            loop(1, 8, lambda k: bwd_copy(0, k).wait_recv())
            send_back(2)

    loop(0, CH, turn)

    def send_quarter(q):
        loop(0, 7, lambda i: quarter_copy(q, first(i)).start())

    def pieces(f, q, grad):
        def pair(m):
            mx, mz = lax.rem(m, 4), m // 4
            rows = aligned(m, 8)
            a, b = grad[2 * q : 2 * q + 2, 0, rows, :], grad[2 * q : 2 * q + 2, 1, rows, :]
            low = low_half()
            rs0[f, 0, mx, q, mz] = jnp.where(low, a, pltpu.roll(b, 4, 1)).reshape(16, 128).astype(BF)
            rs0[f, 1, mx, q, mz] = jnp.where(low, pltpu.roll(a, 4, 1), b).reshape(16, 128).astype(BF)

        loop(0, 16, pair, 4)

    def add_first(f, q):
        for m in range(4):
            total = rs0[f, core, x, q, m].astype(F32)
            for k in range(7):
                total = total + rs_x[f, k, q, m].astype(F32)
            rs2[f, m, q] = total.astype(BF)

    def add_last(f, q, out):
        total = rs2[f, z, q].astype(F32)
        for o in range(3):
            total = total + rs_z[f, o, q].astype(F32)
        out[16 * q : 16 * q + 16, :] = total

    def rx_copy(k):
        px, pc = xc_of(k)
        return remote(rs0.at[1, pc, px], rs_x.at[1, k - 1], rx_s.at[k - 1], rx_r.at[k - 1], xc_peer(k))

    def rz_copy(o):
        return remote(
            rs2.at[1, lax.rem(z + o, 4)], rs_z.at[1, o - 1], rz_s.at[o - 1], rz_r.at[o - 1], z_peer(o)
        )

    def qx_copy(q, k):
        px, pc = xc_of(k)
        return remote(
            rs0.at[0, pc, px, q], rs_x.at[0, k - 1, q], qx_s.at[q, k - 1], qx_r.at[q, k - 1], xc_peer(k)
        )

    def qz_copy(q, o):
        return remote(
            rs2.at[0, lax.rem(z + o, 4), q], rs_z.at[0, o - 1, q],
            qz_s.at[q, o - 1], qz_r.at[q, o - 1], z_peer(o),
        )

    def left_part(c, lo, hi_n):
        def one(n):
            back = brecv[c, :, n].reshape(128, TC).astype(F32)
            dpre = (back * gp[c, n]).astype(BF)
            q, s = n // 2, lax.rem(n, 2)
            lgrad[q, s] = lgrad[q, s] + mm_nt(tokT[c, n], dpre)
            stage3[pl.ds(n, TC, stride=16), :] = mm(lw[n], dpre).T

        loop(lo, hi_n, one, 4)

    def left_out(c):
        def some(i):
            rows = stage3[aligned(i, 256), :].astype(BF).reshape(16, 16, 128)
            tg_out[pl.ds(c * TC + i * 16, 16)] = rows

        loop(0, 8, some)

    def left(c):
        left_part(c, 0, 16)
        left_out(c)

    for q in range(4):
        pieces(1, q, rgrad)
    loop(1, 8, lambda k: rx_copy(k).start())
    left(0)
    loop(1, 8, lambda k: bwd_copy(1, k).wait_recv())
    send_quarter(0)
    send_quarter(1)
    loop(1, 8, lambda k: rx_copy(k).wait_recv())
    for q in range(4):
        add_first(1, q)
    for o in (1, 2, 3):
        rz_copy(o).start()
    left(1)
    loop(1, 8, lambda k: bwd_copy(2, k).wait_recv())
    send_quarter(2)
    left(2)
    for o in (1, 2, 3):
        rz_copy(o).wait_recv()
    for q in range(4):
        add_last(1, q, rg_out)

    def quarter(q):
        loop(1, 8, lambda k: quarter_copy(q, k).wait_recv())
        if q == 0:
            send_quarter(3)
        left_part(LAST, 4 * q, 4 * q + 4)
        pieces(0, q, lgrad)
        loop(1, 8, lambda k: qx_copy(q, k).start())

    def second(q):
        loop(1, 8, lambda k: qx_copy(q, k).wait_recv())
        add_first(0, q)
        for o in (1, 2, 3):
            qz_copy(q, o).start()

    quarter(0)
    quarter(1)
    second(0)
    quarter(2)
    second(1)
    quarter(3)
    second(2)
    left_out(LAST)
    second(3)
    for q in range(4):
        for o in (1, 2, 3):
            qz_copy(q, o).wait_recv()
        add_last(0, q, lg_out)

    for f in (0, 1):
        for h in (0, 1):
            for o in (1, 2, 3):
                ag_z(f, h, o).wait_send()
                ag_x(f, h, o).wait_send()
            for o in (0, 1, 2, 3):
                ag_c(f, h, o).wait_send()
    loop(1, 8, lambda k: rx_copy(k).wait_send())
    for o in (1, 2, 3):
        rz_copy(o).wait_send()

    def drain(c):
        loop(1, 8, lambda k: fwd_copy(c, k).wait_send())

    loop(0, CH, drain)

    def drain_back(c):
        loop(1, 8, lambda k: bwd_copy(c, k).wait_send())

    loop(0, LAST, drain_back)

    def drain_quarter(q):
        loop(1, 8, lambda k: quarter_copy(q, k).wait_send())
        loop(1, 8, lambda k: qx_copy(q, k).wait_send())
        for o in (1, 2, 3):
            qz_copy(q, o).wait_send()

    loop(0, 4, drain_quarter)


def step(tokens, left_factor, right_factor, target):
    V = pltpu.VMEM
    D = pltpu.SemaphoreType.DMA
    hbm = pl.BlockSpec(memory_space=pltpu.HBM)
    vmem = pl.BlockSpec(memory_space=pltpu.VMEM)
    sq = (128, 128)
    scratch = [
        V((CH, TC, 16, 128), BF), V((CH, TC, 16, 128), BF), V((2, 64, 128), F32),
        V((CH, 16, 128, TC), BF), V((CH, 16, 128, TC), BF),
        V((TC * 16, 128), F32), V((16 * 128, TC), F32), V((TC * 16, 128), F32),
        V((2, 2, 2, 4, 4, 32, 128), BF), V((8, 2) + sq, F32),
        V((16,) + sq, BF), V((16,) + sq, BF), V((16,) + sq, BF), V((16,) + sq, BF),
        V((CH, 16, 128, TC), F32),
        V((CH, 8, 16, 16, TC), BF), V((CH, 8, 16, 16, TC), BF),
        V((CH, 8, 16, 16, TC), BF), V((CH, 8, 16, 16, TC), BF),
        V((8, 2) + sq, F32), V((8, 2) + sq, F32),
        V((2, 2, 4, 4, 4, 16, 128), BF), V((2, 7, 4, 4, 16, 128), BF),
        V((2, 4, 4, 16, 128), BF), V((2, 3, 4, 16, 128), BF),
        D((2, CH)), D((2,)),
        D((2, 2, 3)), D((2, 2, 3)), D((2, 2, 3)), D((2, 2, 3)), D((2, 2, 4)), D((2, 2, 4)),
        D((CH, 7)), D((CH, 7)), D((CH, 7)), D((CH, 7)), D((4, 7)), D((4, 7)),
        D((7,)), D((7,)), D((3,)), D((3,)), D((4, 7)), D((4, 7)), D((4, 3)), D((4, 3)),
    ]
    tg, lg, rg = pl.pallas_call(
        kernel,
        name="monarch",
        out_shape=(
            jax.ShapeDtypeStruct((CH * TC, 16, 128), BF),
            jax.ShapeDtypeStruct((64, 128), F32),
            jax.ShapeDtypeStruct((64, 128), F32),
        ),
        in_specs=[hbm, hbm, hbm, hbm],
        out_specs=(vmem, vmem, vmem),
        scratch_shapes=scratch,
        compiler_params=pltpu.CompilerParams(
            collective_id=0, has_side_effects=True, vmem_limit_bytes=51 << 20
        ),
    )(tokens, left_factor.reshape(64, 128), right_factor.reshape(64, 128), target)
    return tg, lg.reshape(16, 4, 128), rg.reshape(16, 4, 128)


def solution(mesh):
    in_specs = (P("dp", "mp", None), P("mp", "dp", None), P("mp", "dp", None), P("dp", "mp", None))
    out_specs = (P("dp", "mp", None), P("mp", "dp", None), P("mp", "dp", None))
    return jax.shard_map(step, mesh=mesh, in_specs=in_specs, out_specs=out_specs, check_vma=False)
```

```python
import jax
import jax.numpy as jnp
from jax import lax
from jax.experimental import pallas as pl
from jax.experimental.pallas import tpu as pltpu
from jax.sharding import PartitionSpec as P

MESH = pl.DeviceIdType.MESH
BF, F32 = jnp.bfloat16, jnp.float32
CH = 4
TC = 128
LAST = CH - 1
GELU_K = 0.7978845608028654
GELU_C = 0.044715


def mm(a, b):
    return jnp.dot(a, b, preferred_element_type=F32)


def mm_nt(a, b):
    return lax.dot_general(a, b, (((1,), (1,)), ((), ())), preferred_element_type=F32)


def loop(lo, hi, body, unroll=1):
    def step(i, carry):
        body(i)
        return carry

    lax.fori_loop(lo, hi, step, 0, unroll=unroll)


def aligned(i, size):
    return pl.ds(pl.multiple_of(i * size, size), size)


def low_half():
    return lax.broadcasted_iota(jnp.int32, (1, 8, 128), 1) < 4


def kernel(
    tok_hbm, w_ref, tgt_hbm,
    tg_out, lg_out, rg_out,
    tok_raw, tgt_raw, tokT, tgtT, stage, stage2, stage3,
    gath, wfull, lw, lwT, rw, rwT,
    gp, fsend, frecv, bsend, brecv, lgrad, rgrad,
    rs0, rs_x, rs2, rs_z,
    in_sem, agz_s, agz_r, agx_s, agx_r, agc_s, agc_r,
    f_s, f_r, b_s, b_r, q_s, q_r, rx_s, rx_r, rz_s, rz_r, qx_s, qx_r, qz_s, qz_r,
):
    dp, mp = lax.axis_index("dp"), lax.axis_index("mp")
    z, x, core = dp // 8, lax.rem(dp // 2, 4), lax.rem(dp, 2)
    hi, y = mp // 4, lax.rem(mp, 4)

    def z_peer(o):
        return (lax.rem(z + o, 4) * 8 + x * 2 + core, mp)

    def xc_of(k):
        return lax.rem(x + lax.rem(k, 4), 4), lax.rem(core + k // 4, 2)

    def xc_peer(k):
        px, pc = xc_of(k)
        return (z * 8 + px * 2 + pc, mp)

    def m_of(k):
        return lax.rem(hi + k // 4, 2) * 4 + lax.rem(y + lax.rem(k, 4), 4)

    def remote(src, dst, ss, rs, dev):
        return pltpu.make_async_remote_copy(
            src_ref=src, dst_ref=dst, send_sem=ss, recv_sem=rs, device_id=dev, device_id_type=MESH
        )

    barrier = pltpu.get_barrier_semaphore()
    peers = [z_peer(o) for o in (1, 2, 3)] + [xc_peer(k) for k in range(1, 8)]
    peers += [(dp, m_of(k)) for k in range(1, 8)]
    for dev in peers:
        pl.semaphore_signal(barrier, inc=1, device_id=dev, device_id_type=MESH)

    def tok_in(c):
        return pltpu.make_async_copy(tok_hbm.at[aligned(c, TC)], tok_raw.at[c], in_sem.at[0, c])

    def tgt_in(c):
        return pltpu.make_async_copy(tgt_hbm.at[aligned(c, TC)], tgt_raw.at[c], in_sem.at[1, c])

    loop(0, CH, lambda c: tok_in(c).start())
    loop(0, CH, lambda c: tgt_in(c).start())
    for f in (0, 1):
        for h in (0, 1):
            gath[f, h, core, x, z] = w_ref[f, h]
    pl.semaphore_wait(barrier, len(peers))

    def ag_z(f, h, o):
        piece = gath.at[f, h, core, x, z]
        return remote(piece, piece, agz_s.at[f, h, o - 1], agz_r.at[f, h, o - 1], z_peer(o))

    def ag_x(f, h, o):
        piece = gath.at[f, h, core, x]
        return remote(piece, piece, agx_s.at[f, h, o - 1], agx_r.at[f, h, o - 1], xc_peer(o))

    def ag_c(f, h, o):
        piece = gath.at[f, h, core, lax.rem(x + 4 - o, 4)]
        return remote(piece, piece, agc_s.at[f, h, o], agc_r.at[f, h, o], xc_peer(4))

    def gather_first(f, h):
        for o in (1, 2, 3):
            ag_z(f, h, o).start()

    def gather_second(f, h):
        for o in (1, 2, 3):
            ag_z(f, h, o).wait_recv()
        for o in (1, 2, 3):
            ag_x(f, h, o).start()
        ag_c(f, h, 0).start()

    def gather_third(f, h):
        for o in (1, 2, 3):
            ag_x(f, h, o).wait_recv()
            ag_c(f, h, o).start()

    def gather_end(f, h):
        for o in (0, 1, 2, 3):
            ag_c(f, h, o).wait_recv()

    def spread(raw, outT, c):
        stage[...] = raw[c].astype(F32).reshape(TC * 16, 128)

        def one(n):
            rows = stage[pl.ds(n, TC, stride=16), :]
            outT[c, n] = rows.T.astype(BF)

        loop(0, 16, one, 4)

    def tokens_ready(c):
        tok_in(c).wait()
        spread(tok_raw, tokT, c)

    def targets_ready(c):
        tgt_in(c).wait()
        spread(tgt_raw, tgtT, c)

    def assemble(f, h, w, wT):
        def pair(m):
            mx, mz = lax.rem(m, 4), m // 4
            a = gath[f, h, 0, mx, mz].astype(F32).reshape(4, 8, 128)
            b = gath[f, h, 1, mx, mz].astype(F32).reshape(4, 8, 128)
            low = low_half()
            rows = aligned(m, 8)
            wfull[4 * h : 4 * h + 4, 0, rows, :] = jnp.where(low, a, pltpu.roll(b, 4, 1))
            wfull[4 * h : 4 * h + 4, 1, rows, :] = jnp.where(low, pltpu.roll(a, 4, 1), b)

        loop(0, 16, pair, 4)

        def one(n):
            full = wfull[n // 2, lax.rem(n, 2)]
            w[n] = full.astype(BF)
            wT[n] = full.T.astype(BF)

        loop(8 * h, 8 * h + 8, one, 4)

    def fwd_copy(c, k):
        return remote(
            fsend.at[c, m_of(k)], frecv.at[c, mp], f_s.at[c, k - 1], f_r.at[c, k - 1], (dp, m_of(k))
        )

    def bwd_copy(c, k):
        return remote(
            bsend.at[c, m_of(k)], brecv.at[c, mp], b_s.at[c, k - 1], b_r.at[c, k - 1], (dp, m_of(k))
        )

    def quarter_copy(q, k):
        part = pl.ds(4 * q, 4)
        return remote(
            bsend.at[LAST, m_of(k), part], brecv.at[LAST, mp, part],
            q_s.at[q, k - 1], q_r.at[q, k - 1], (dp, m_of(k)),
        )

    def regroup(src, g, m):
        return src[pl.ds(g * 16 + m, 16, stride=128), :].astype(BF)

    def forward_part(c, jh, lo, hi_n):
        rows = aligned(jh, 64)

        def one(n):
            pre = mm(lwT[n, rows, :], tokT[c, n])
            sq = pre * pre
            th = jnp.tanh(pre * (GELU_K + (GELU_K * GELU_C) * sq))
            half = 0.5 + 0.5 * th
            gp[c, n, rows, :] = half + (0.5 * pre) * (1.0 - th * th) * (
                GELU_K + (3.0 * GELU_K * GELU_C) * sq
            )
            stage2[pl.ds(pl.multiple_of(n * 128 + jh * 64, 64), 64), :] = pre * half

        loop(lo, hi_n, one, 4)

    def forward_send(c, lo, hi_k):
        def send(k):
            g = m_of(k)
            for m in range(16):
                fsend[c, g, m] = regroup(stage2, g, m)
            fwd_copy(c, k).start()

        loop(lo, hi_k, send)

    def forward_rest(c):
        forward_part(c, hi, 0, 16)
        forward_send(c, 1, 4)
        for m in range(16):
            frecv[c, mp, m] = regroup(stage2, mp, m)

    for h in (0, 1):
        gather_first(0, h)
    tokens_ready(0)
    for h in (0, 1):
        gather_second(0, h)
    for h in (0, 1):
        gather_first(1, h)
    tokens_ready(1)
    for h in (0, 1):
        gather_third(0, h)
    for h in (0, 1):
        gather_second(1, h)
    for h in (0, 1):
        gather_end(0, h)
        assemble(0, h, lw, lwT)
        forward_part(0, 1 - hi, 8 * h, 8 * h + 8)
    forward_send(0, 4, 8)
    forward_rest(0)

    def forward(c):
        forward_part(c, 1 - hi, 0, 16)
        forward_send(c, 4, 8)
        forward_rest(c)

    forward(1)
    for h in (0, 1):
        gather_third(1, h)

    for h in (0, 1):
        gather_end(1, h)
        assemble(1, h, rw, rwT)

    lgrad[...] = jnp.zeros_like(lgrad)
    rgrad[...] = jnp.zeros_like(rgrad)

    def right(c):
        def one(n):
            act = frecv[c, :, n].reshape(128, TC)
            out = mm(rwT[n], act)
            dout = (out - tgtT[c, n].astype(F32)).astype(BF)
            q, s = n // 2, lax.rem(n, 2)
            rgrad[q, s] = rgrad[q, s] + mm_nt(act, dout)
            stage2[aligned(n, 128), :] = mm(rw[n], dout)

        loop(0, 16, one, 4)
        for m in range(16):
            brecv[c, mp, m] = regroup(stage2, mp, m)

        def fill(k):
            g = m_of(k)
            for m in range(16):
                bsend[c, g, m] = regroup(stage2, g, m)

        loop(1, 8, fill)

    def first(i):
        return lax.rem(i + 3, 7) + 1

    def send_back(c):
        loop(0, 7, lambda i: bwd_copy(c, first(i)).start())

    def sent(copy, u):
        loop(1, 8, lambda k: copy(u, k).wait_send())

    def turn(c):
        targets_ready(c)

        @pl.when(c < 2)
        def _():
            tokens_ready(c + 2)
            sent(fwd_copy, 2 * c)
            forward(c + 2)

        loop(1, 8, lambda k: fwd_copy(c, k).wait_recv())
        right(c)

        @pl.when(c == 0)
        def _():
            sent(fwd_copy, 1)
            send_back(0)

        @pl.when(c == 1)
        def _():
            sent(bwd_copy, 0)
            send_back(1)

        @pl.when(c == 2)
        def _():
            sent(fwd_copy, 3)
            send_back(2)

    loop(0, CH, turn)

    def send_quarter(q):
        loop(0, 7, lambda i: quarter_copy(q, first(i)).start())

    def pieces(f, q, grad):
        def pair(m):
            mx, mz = lax.rem(m, 4), m // 4
            rows = aligned(m, 8)
            a, b = grad[2 * q : 2 * q + 2, 0, rows, :], grad[2 * q : 2 * q + 2, 1, rows, :]
            low = low_half()
            rs0[f, 0, mx, q, mz] = jnp.where(low, a, pltpu.roll(b, 4, 1)).reshape(16, 128).astype(BF)
            rs0[f, 1, mx, q, mz] = jnp.where(low, pltpu.roll(a, 4, 1), b).reshape(16, 128).astype(BF)

        loop(0, 16, pair, 4)

    def add_first(f, q):
        for m in range(4):
            total = rs0[f, core, x, q, m].astype(F32)
            for k in range(7):
                total = total + rs_x[f, k, q, m].astype(F32)
            rs2[f, m, q] = total.astype(BF)

    def add_last(f, q, out):
        total = rs2[f, z, q].astype(F32)
        for o in range(3):
            total = total + rs_z[f, o, q].astype(F32)
        out[16 * q : 16 * q + 16, :] = total

    def rx_copy(k):
        px, pc = xc_of(k)
        return remote(rs0.at[1, pc, px], rs_x.at[1, k - 1], rx_s.at[k - 1], rx_r.at[k - 1], xc_peer(k))

    def rz_copy(o):
        return remote(
            rs2.at[1, lax.rem(z + o, 4)], rs_z.at[1, o - 1], rz_s.at[o - 1], rz_r.at[o - 1], z_peer(o)
        )

    def qx_copy(q, k):
        px, pc = xc_of(k)
        return remote(
            rs0.at[0, pc, px, q], rs_x.at[0, k - 1, q], qx_s.at[q, k - 1], qx_r.at[q, k - 1], xc_peer(k)
        )

    def qz_copy(q, o):
        return remote(
            rs2.at[0, lax.rem(z + o, 4), q], rs_z.at[0, o - 1, q],
            qz_s.at[q, o - 1], qz_r.at[q, o - 1], z_peer(o),
        )

    def left_part(c, lo, hi_n):
        def one(n):
            back = brecv[c, :, n].reshape(128, TC).astype(F32)
            dpre = (back * gp[c, n]).astype(BF)
            q, s = n // 2, lax.rem(n, 2)
            lgrad[q, s] = lgrad[q, s] + mm_nt(tokT[c, n], dpre)
            stage3[pl.ds(n, TC, stride=16), :] = mm(lw[n], dpre).T

        loop(lo, hi_n, one, 4)

    def left_out(c):
        def some(i):
            rows = stage3[aligned(i, 256), :].astype(BF).reshape(16, 16, 128)
            tg_out[pl.ds(c * TC + i * 16, 16)] = rows

        loop(0, 8, some)

    def left(c):
        left_part(c, 0, 16)
        left_out(c)

    for q in range(4):
        pieces(1, q, rgrad)
    loop(1, 8, lambda k: rx_copy(k).start())
    loop(1, 8, lambda k: bwd_copy(0, k).wait_recv())
    left(0)
    sent(bwd_copy, 1)
    send_quarter(0)
    send_quarter(1)
    send_quarter(2)
    loop(1, 8, lambda k: bwd_copy(1, k).wait_recv())
    loop(1, 8, lambda k: rx_copy(k).wait_recv())
    for q in range(4):
        add_first(1, q)
    for o in (1, 2, 3):
        rz_copy(o).start()
    left(1)
    sent(bwd_copy, 2)
    loop(1, 8, lambda k: bwd_copy(2, k).wait_recv())
    left(2)
    for o in (1, 2, 3):
        rz_copy(o).wait_recv()
    for q in range(4):
        add_last(1, q, rg_out)

    def quarter(q):
        if q == 0:
            sent(quarter_copy, 0)
            send_quarter(3)
        loop(1, 8, lambda k: quarter_copy(q, k).wait_recv())
        left_part(LAST, 4 * q, 4 * q + 4)
        pieces(0, q, lgrad)
        loop(1, 8, lambda k: qx_copy(q, k).start())

    def second(q):
        loop(1, 8, lambda k: qx_copy(q, k).wait_recv())
        add_first(0, q)
        for o in (1, 2, 3):
            qz_copy(q, o).start()

    for q in range(4):
        quarter(q)
    second(0)
    second(1)
    second(2)
    left_out(LAST)
    second(3)
    for q in range(4):
        for o in (1, 2, 3):
            qz_copy(q, o).wait_recv()
        add_last(0, q, lg_out)

    for f in (0, 1):
        for h in (0, 1):
            for o in (1, 2, 3):
                ag_z(f, h, o).wait_send()
                ag_x(f, h, o).wait_send()
            for o in (0, 1, 2, 3):
                ag_c(f, h, o).wait_send()
    loop(1, 8, lambda k: rx_copy(k).wait_send())
    for o in (1, 2, 3):
        rz_copy(o).wait_send()

    def drain_quarter(q):
        loop(1, 8, lambda k: qx_copy(q, k).wait_send())
        for o in (1, 2, 3):
            qz_copy(q, o).wait_send()

    loop(0, 4, drain_quarter)
    loop(1, 4, lambda q: sent(quarter_copy, q))


def step(tokens, left_factor, right_factor, target):
    V = pltpu.VMEM
    D = pltpu.SemaphoreType.DMA
    hbm = pl.BlockSpec(memory_space=pltpu.HBM)
    vmem = pl.BlockSpec(memory_space=pltpu.VMEM)
    sq = (128, 128)
    scratch = [
        V((CH, TC, 16, 128), BF), V((CH, TC, 16, 128), BF),
        V((CH, 16, 128, TC), BF), V((CH, 16, 128, TC), BF),
        V((TC * 16, 128), F32), V((16 * 128, TC), F32), V((TC * 16, 128), F32),
        V((2, 2, 2, 4, 4, 32, 128), BF), V((8, 2) + sq, F32),
        V((16,) + sq, BF), V((16,) + sq, BF), V((16,) + sq, BF), V((16,) + sq, BF),
        V((CH, 16, 128, TC), F32),
        V((CH, 8, 16, 16, TC), BF), V((CH, 8, 16, 16, TC), BF),
        V((CH, 8, 16, 16, TC), BF), V((CH, 8, 16, 16, TC), BF),
        V((8, 2) + sq, F32), V((8, 2) + sq, F32),
        V((2, 2, 4, 4, 4, 16, 128), BF), V((2, 7, 4, 4, 16, 128), BF),
        V((2, 4, 4, 16, 128), BF), V((2, 3, 4, 16, 128), BF),
        D((2, CH)),
        D((2, 2, 3)), D((2, 2, 3)), D((2, 2, 3)), D((2, 2, 3)), D((2, 2, 4)), D((2, 2, 4)),
        D((CH, 7)), D((CH, 7)), D((CH, 7)), D((CH, 7)), D((4, 7)), D((4, 7)),
        D((7,)), D((7,)), D((3,)), D((3,)), D((4, 7)), D((4, 7)), D((4, 3)), D((4, 3)),
    ]
    which = lax.broadcasted_iota(jnp.int32, (2, 16, 4, 128), 0)
    factors = jnp.where(which == 0, left_factor[None], right_factor[None])
    factors = factors.astype(BF).reshape(2, 2, 32, 128)
    tg, lg, rg = pl.pallas_call(
        kernel,
        name="monarch",
        out_shape=(
            jax.ShapeDtypeStruct((CH * TC, 16, 128), BF),
            jax.ShapeDtypeStruct((64, 128), F32),
            jax.ShapeDtypeStruct((64, 128), F32),
        ),
        in_specs=[hbm, vmem, hbm],
        out_specs=(vmem, vmem, vmem),
        scratch_shapes=scratch,
        compiler_params=pltpu.CompilerParams(
            collective_id=0, has_side_effects=True, vmem_limit_bytes=51 << 20
        ),
    )(tokens, factors, target)
    return tg, lg.reshape(16, 4, 128), rg.reshape(16, 4, 128)


def solution(mesh):
    in_specs = (P("dp", "mp", None), P("mp", "dp", None), P("mp", "dp", None), P("dp", "mp", None))
    out_specs = (P("dp", "mp", None), P("mp", "dp", None), P("mp", "dp", None))
    return jax.shard_map(step, mesh=mesh, in_specs=in_specs, out_specs=out_specs, check_vma=False)
```

```python
import jax
import jax.numpy as jnp
from jax import lax
from jax.experimental import pallas as pl
from jax.experimental.pallas import tpu as pltpu
from jax.sharding import PartitionSpec as P

MESH = pl.DeviceIdType.MESH
BF, F32 = jnp.bfloat16, jnp.float32
CH = 4
TC = 128
LAST = CH - 1
GELU_K = 0.7978845608028654
GELU_C = 0.044715


def mm(a, b):
    return jnp.dot(a, b, preferred_element_type=F32)


def mm_nt(a, b):
    return lax.dot_general(a, b, (((1,), (1,)), ((), ())), preferred_element_type=F32)


def loop(lo, hi, body, unroll=1):
    def step(i, carry):
        body(i)
        return carry

    lax.fori_loop(lo, hi, step, 0, unroll=unroll)


def aligned(i, size):
    return pl.ds(pl.multiple_of(i * size, size), size)


def low_half():
    return lax.broadcasted_iota(jnp.int32, (1, 8, 128), 1) < 4


def kernel(
    tok_hbm, w_ref, tgt_hbm,
    tg_out, grads_out,
    tok_raw, tgt_raw, tokT, tgtT, stage, stage2, stage3,
    gath, wfull, lw, lwT, rw, rwT,
    gp, fsend, frecv, bsend, brecv, lgrad, rgrad,
    rs0, rs_x, rs2, rs_z,
    in_sem, agz_s, agz_r, agx_s, agx_r, agc_s, agc_r,
    f_s, f_r, b_s, b_r, q_s, q_r, rx_s, rx_r, rz_s, rz_r, qx_s, qx_r, qz_s, qz_r,
):
    dp, mp = lax.axis_index("dp"), lax.axis_index("mp")
    z, x, core = dp // 8, lax.rem(dp // 2, 4), lax.rem(dp, 2)
    hi, y = mp // 4, lax.rem(mp, 4)

    def z_peer(o):
        return (lax.rem(z + o, 4) * 8 + x * 2 + core, mp)

    def xc_of(k):
        return lax.rem(x + lax.rem(k, 4), 4), lax.rem(core + k // 4, 2)

    def xc_peer(k):
        px, pc = xc_of(k)
        return (z * 8 + px * 2 + pc, mp)

    def m_of(k):
        return lax.rem(hi + k // 4, 2) * 4 + lax.rem(y + lax.rem(k, 4), 4)

    def remote(src, dst, ss, rs, dev):
        return pltpu.make_async_remote_copy(
            src_ref=src, dst_ref=dst, send_sem=ss, recv_sem=rs, device_id=dev, device_id_type=MESH
        )

    barrier = pltpu.get_barrier_semaphore()
    peers = [z_peer(o) for o in (1, 2, 3)] + [xc_peer(k) for k in range(1, 8)]
    peers += [(dp, m_of(k)) for k in range(1, 8)]
    for dev in peers:
        pl.semaphore_signal(barrier, inc=1, device_id=dev, device_id_type=MESH)

    def tok_in(c):
        return pltpu.make_async_copy(tok_hbm.at[aligned(c, TC)], tok_raw.at[c], in_sem.at[0, c])

    def tgt_in(c):
        return pltpu.make_async_copy(tgt_hbm.at[aligned(c, TC)], tgt_raw.at[c], in_sem.at[1, c])

    loop(0, CH, lambda c: tok_in(c).start())
    loop(0, CH, lambda c: tgt_in(c).start())
    for f in (0, 1):
        for h in (0, 1):
            gath[f, h, core, x, z] = w_ref[f, h]
    pl.semaphore_wait(barrier, len(peers))

    def ag_z(f, h, o):
        piece = gath.at[f, h, core, x, z]
        return remote(piece, piece, agz_s.at[f, h, o - 1], agz_r.at[f, h, o - 1], z_peer(o))

    def ag_x(f, h, o):
        piece = gath.at[f, h, core, x]
        return remote(piece, piece, agx_s.at[f, h, o - 1], agx_r.at[f, h, o - 1], xc_peer(o))

    def ag_c(f, h, o):
        piece = gath.at[f, h, core, lax.rem(x + 4 - o, 4)]
        return remote(piece, piece, agc_s.at[f, h, o], agc_r.at[f, h, o], xc_peer(4))

    def gather_first(f, h):
        for o in (1, 2, 3):
            ag_z(f, h, o).start()

    def gather_second(f, h):
        for o in (1, 2, 3):
            ag_z(f, h, o).wait_recv()
        for o in (1, 2, 3):
            ag_x(f, h, o).start()
        ag_c(f, h, 0).start()

    def gather_third(f, h):
        for o in (1, 2, 3):
            ag_x(f, h, o).wait_recv()
            ag_c(f, h, o).start()

    def gather_end(f, h):
        for o in (0, 1, 2, 3):
            ag_c(f, h, o).wait_recv()

    def spread(raw, outT, c):
        stage[...] = raw[c].astype(F32).reshape(TC * 16, 128)

        def one(n):
            rows = stage[pl.ds(n, TC, stride=16), :]
            outT[c, n] = rows.T.astype(BF)

        loop(0, 16, one, 4)

    def tokens_ready(c):
        tok_in(c).wait()
        spread(tok_raw, tokT, c)

    def targets_ready(c):
        tgt_in(c).wait()
        spread(tgt_raw, tgtT, c)

    def assemble(f, h, w, wT):
        def pair(m):
            mx, mz = lax.rem(m, 4), m // 4
            a = gath[f, h, 0, mx, mz].astype(F32).reshape(4, 8, 128)
            b = gath[f, h, 1, mx, mz].astype(F32).reshape(4, 8, 128)
            low = low_half()
            rows = aligned(m, 8)
            wfull[4 * h : 4 * h + 4, 0, rows, :] = jnp.where(low, a, pltpu.roll(b, 4, 1))
            wfull[4 * h : 4 * h + 4, 1, rows, :] = jnp.where(low, pltpu.roll(a, 4, 1), b)

        loop(0, 16, pair, 4)

        def one(n):
            full = wfull[n // 2, lax.rem(n, 2)]
            w[n] = full.astype(BF)
            wT[n] = full.T.astype(BF)

        loop(8 * h, 8 * h + 8, one, 4)

    def fwd_copy(c, k):
        return remote(
            fsend.at[c, m_of(k)], frecv.at[c, mp], f_s.at[c, k - 1], f_r.at[c, k - 1], (dp, m_of(k))
        )

    def bwd_copy(c, k):
        return remote(
            bsend.at[c, m_of(k)], brecv.at[c, mp], b_s.at[c, k - 1], b_r.at[c, k - 1], (dp, m_of(k))
        )

    def quarter_copy(q, k):
        part = pl.ds(4 * q, 4)
        return remote(
            bsend.at[LAST, m_of(k), part], brecv.at[LAST, mp, part],
            q_s.at[q, k - 1], q_r.at[q, k - 1], (dp, m_of(k)),
        )

    def regroup(src, g, m):
        return src[pl.ds(g * 16 + m, 16, stride=128), :].astype(BF)

    def forward_part(c, jh, lo, hi_n):
        rows = aligned(jh, 64)

        def one(n):
            pre = mm(lwT[n, rows, :], tokT[c, n])
            sq = pre * pre
            th = jnp.tanh(pre * (GELU_K + (GELU_K * GELU_C) * sq))
            half = 0.5 + 0.5 * th
            gp[c, n, rows, :] = half + (0.5 * pre) * (1.0 - th * th) * (
                GELU_K + (3.0 * GELU_K * GELU_C) * sq
            )
            stage2[pl.ds(pl.multiple_of(n * 128 + jh * 64, 64), 64), :] = pre * half

        loop(lo, hi_n, one, 4)

    def forward_send(c, lo, hi_k):
        def send(k):
            g = m_of(k)
            for m in range(16):
                fsend[c, g, m] = regroup(stage2, g, m)
            fwd_copy(c, k).start()

        loop(lo, hi_k, send)

    def forward_rest(c):
        forward_part(c, hi, 0, 16)
        forward_send(c, 1, 4)
        for m in range(16):
            frecv[c, mp, m] = regroup(stage2, mp, m)

    for h in (0, 1):
        gather_first(0, h)
    tokens_ready(0)
    for h in (0, 1):
        gather_second(0, h)
    for h in (0, 1):
        gather_first(1, h)
    tokens_ready(1)
    for h in (0, 1):
        gather_third(0, h)
    for h in (0, 1):
        gather_second(1, h)
    for h in (0, 1):
        gather_end(0, h)
        assemble(0, h, lw, lwT)
        forward_part(0, 1 - hi, 8 * h, 8 * h + 8)
    forward_send(0, 4, 8)
    forward_rest(0)

    def forward(c):
        forward_part(c, 1 - hi, 0, 16)
        forward_send(c, 4, 8)
        forward_rest(c)

    forward(1)
    for h in (0, 1):
        gather_third(1, h)

    for h in (0, 1):
        gather_end(1, h)
        assemble(1, h, rw, rwT)

    lgrad[...] = jnp.zeros_like(lgrad)
    rgrad[...] = jnp.zeros_like(rgrad)

    def right(c):
        def one(n):
            act = frecv[c, :, n].reshape(128, TC)
            out = mm(rwT[n], act)
            dout = (out - tgtT[c, n].astype(F32)).astype(BF)
            q, s = n // 2, lax.rem(n, 2)
            rgrad[q, s] = rgrad[q, s] + mm_nt(act, dout)
            stage2[aligned(n, 128), :] = mm(rw[n], dout)

        loop(0, 16, one, 4)
        for m in range(16):
            brecv[c, mp, m] = regroup(stage2, mp, m)

        def fill(k):
            g = m_of(k)
            for m in range(16):
                bsend[c, g, m] = regroup(stage2, g, m)

        loop(1, 8, fill)

    def first(i):
        return lax.rem(i + 3, 7) + 1

    def send_back(c):
        loop(0, 7, lambda i: bwd_copy(c, first(i)).start())

    def sent(copy, u):
        loop(1, 8, lambda k: copy(u, k).wait_send())

    def turn(c):
        targets_ready(c)

        @pl.when(c < 2)
        def _():
            tokens_ready(c + 2)
            sent(fwd_copy, 2 * c)
            forward(c + 2)

        loop(1, 8, lambda k: fwd_copy(c, k).wait_recv())
        right(c)

        @pl.when(c == 0)
        def _():
            sent(fwd_copy, 1)
            send_back(0)

        @pl.when(c == 1)
        def _():
            sent(bwd_copy, 0)
            send_back(1)

        @pl.when(c == 2)
        def _():
            sent(fwd_copy, 3)
            send_back(2)

    loop(0, CH, turn)

    def send_quarter(q):
        loop(0, 7, lambda i: quarter_copy(q, first(i)).start())

    def pieces(f, q, grad):
        def pair(m):
            mx, mz = lax.rem(m, 4), m // 4
            rows = aligned(m, 8)
            a, b = grad[2 * q : 2 * q + 2, 0, rows, :], grad[2 * q : 2 * q + 2, 1, rows, :]
            low = low_half()
            rs0[f, 0, mx, q, mz] = jnp.where(low, a, pltpu.roll(b, 4, 1)).reshape(16, 128).astype(BF)
            rs0[f, 1, mx, q, mz] = jnp.where(low, pltpu.roll(a, 4, 1), b).reshape(16, 128).astype(BF)

        loop(0, 16, pair, 4)

    def add_first(f, q):
        for m in range(4):
            total = rs0[f, core, x, q, m].astype(F32)
            for k in range(7):
                total = total + rs_x[f, k, q, m].astype(F32)
            rs2[f, m, q] = total.astype(BF)

    def add_last(f, q, out):
        total = rs2[f, z, q].astype(F32)
        for o in range(3):
            total = total + rs_z[f, o, q].astype(F32)
        out[16 * q : 16 * q + 16, :] = total

    def rx_copy(k):
        px, pc = xc_of(k)
        return remote(rs0.at[1, pc, px], rs_x.at[1, k - 1], rx_s.at[k - 1], rx_r.at[k - 1], xc_peer(k))

    def rz_copy(o):
        return remote(
            rs2.at[1, lax.rem(z + o, 4)], rs_z.at[1, o - 1], rz_s.at[o - 1], rz_r.at[o - 1], z_peer(o)
        )

    def qx_copy(q, k):
        px, pc = xc_of(k)
        return remote(
            rs0.at[0, pc, px, q], rs_x.at[0, k - 1, q], qx_s.at[q, k - 1], qx_r.at[q, k - 1], xc_peer(k)
        )

    def qz_copy(q, o):
        return remote(
            rs2.at[0, lax.rem(z + o, 4), q], rs_z.at[0, o - 1, q],
            qz_s.at[q, o - 1], qz_r.at[q, o - 1], z_peer(o),
        )

    def left_part(c, lo, hi_n):
        def one(n):
            back = brecv[c, :, n].reshape(128, TC).astype(F32)
            dpre = (back * gp[c, n]).astype(BF)
            q, s = n // 2, lax.rem(n, 2)
            lgrad[q, s] = lgrad[q, s] + mm_nt(tokT[c, n], dpre)
            stage3[pl.ds(n, TC, stride=16), :] = mm(lw[n], dpre).T

        loop(lo, hi_n, one, 4)

    def left_out(c):
        def some(i):
            rows = stage3[aligned(i, 256), :].astype(BF).reshape(16, 16, 128)
            tg_out[pl.ds(c * TC + i * 16, 16)] = rows

        loop(0, 8, some)

    def left(c):
        left_part(c, 0, 16)
        left_out(c)

    for q in range(4):
        pieces(1, q, rgrad)
    loop(1, 8, lambda k: rx_copy(k).start())
    loop(1, 8, lambda k: bwd_copy(0, k).wait_recv())
    left(0)
    sent(bwd_copy, 1)
    send_quarter(0)
    send_quarter(1)
    send_quarter(2)
    loop(1, 8, lambda k: bwd_copy(1, k).wait_recv())
    loop(1, 8, lambda k: rx_copy(k).wait_recv())
    for q in range(4):
        add_first(1, q)
    for o in (1, 2, 3):
        rz_copy(o).start()
    left(1)
    for f in (0, 1):
        for h in (0, 1):
            for o in (1, 2, 3):
                ag_z(f, h, o).wait_send()
                ag_x(f, h, o).wait_send()
            for o in (0, 1, 2, 3):
                ag_c(f, h, o).wait_send()
    loop(1, 8, lambda k: rx_copy(k).wait_send())
    sent(bwd_copy, 2)
    loop(1, 8, lambda k: bwd_copy(2, k).wait_recv())
    left(2)
    for o in (1, 2, 3):
        rz_copy(o).wait()
    for q in range(4):
        add_last(1, q, grads_out.at[1])

    def quarter(q):
        if q == 0:
            sent(quarter_copy, 0)
            send_quarter(3)
        loop(1, 8, lambda k: quarter_copy(q, k).wait_recv())
        left_part(LAST, 4 * q, 4 * q + 4)
        pieces(0, q, lgrad)
        loop(1, 8, lambda k: qx_copy(q, k).start())

    def second(q):
        loop(1, 8, lambda k: qx_copy(q, k).wait_recv())
        add_first(0, q)
        for o in (1, 2, 3):
            qz_copy(q, o).start()

    for q in range(4):
        quarter(q)
    second(0)
    second(1)
    second(2)
    left_out(LAST)
    loop(1, 4, lambda q: sent(quarter_copy, q))
    loop(0, 3, lambda q: sent(qx_copy, q))
    second(3)
    for q in range(4):
        for o in (1, 2, 3):
            qz_copy(q, o).wait_recv()
        add_last(0, q, grads_out.at[0])

    sent(qx_copy, 3)
    for q in range(4):
        for o in (1, 2, 3):
            qz_copy(q, o).wait_send()


def step(tokens, left_factor, right_factor, target):
    V = pltpu.VMEM
    D = pltpu.SemaphoreType.DMA
    hbm = pl.BlockSpec(memory_space=pltpu.HBM)
    vmem = pl.BlockSpec(memory_space=pltpu.VMEM)
    sq = (128, 128)
    scratch = [
        V((CH, TC, 16, 128), BF), V((CH, TC, 16, 128), BF),
        V((CH, 16, 128, TC), BF), V((CH, 16, 128, TC), BF),
        V((TC * 16, 128), F32), V((16 * 128, TC), F32), V((TC * 16, 128), F32),
        V((2, 2, 2, 4, 4, 32, 128), BF), V((8, 2) + sq, F32),
        V((16,) + sq, BF), V((16,) + sq, BF), V((16,) + sq, BF), V((16,) + sq, BF),
        V((CH, 16, 128, TC), F32),
        V((CH, 8, 16, 16, TC), BF), V((CH, 8, 16, 16, TC), BF),
        V((CH, 8, 16, 16, TC), BF), V((CH, 8, 16, 16, TC), BF),
        V((8, 2) + sq, F32), V((8, 2) + sq, F32),
        V((2, 2, 4, 4, 4, 16, 128), BF), V((2, 7, 4, 4, 16, 128), BF),
        V((2, 4, 4, 16, 128), BF), V((2, 3, 4, 16, 128), BF),
        D((2, CH)),
        D((2, 2, 3)), D((2, 2, 3)), D((2, 2, 3)), D((2, 2, 3)), D((2, 2, 4)), D((2, 2, 4)),
        D((CH, 7)), D((CH, 7)), D((CH, 7)), D((CH, 7)), D((4, 7)), D((4, 7)),
        D((7,)), D((7,)), D((3,)), D((3,)), D((4, 7)), D((4, 7)), D((4, 3)), D((4, 3)),
    ]
    which = lax.broadcasted_iota(jnp.int32, (2, 16, 4, 128), 0)
    factors = jnp.where(which == 0, left_factor[None], right_factor[None])
    factors = factors.astype(BF).reshape(2, 2, 32, 128)
    tg, grads = pl.pallas_call(
        kernel,
        name="monarch",
        out_shape=(
            jax.ShapeDtypeStruct((CH * TC, 16, 128), BF),
            jax.ShapeDtypeStruct((2, 64, 128), F32),
        ),
        in_specs=[hbm, vmem, hbm],
        out_specs=(vmem, vmem),
        scratch_shapes=scratch,
        compiler_params=pltpu.CompilerParams(
            collective_id=0, has_side_effects=True, vmem_limit_bytes=51 << 20
        ),
    )(tokens, factors, target)
    lg, rg = grads.reshape(2, 16, 4, 128)
    return tg, lg, rg


def solution(mesh):
    in_specs = (P("dp", "mp", None), P("mp", "dp", None), P("mp", "dp", None), P("dp", "mp", None))
    out_specs = (P("dp", "mp", None), P("mp", "dp", None), P("mp", "dp", None))
    return jax.shard_map(step, mesh=mesh, in_specs=in_specs, out_specs=out_specs, check_vma=False)
```

```python
import jax
import jax.numpy as jnp
from jax import lax
from jax.experimental import pallas as pl
from jax.experimental.pallas import tpu as pltpu
from jax.sharding import PartitionSpec as P

MESH = pl.DeviceIdType.MESH
BF, F32 = jnp.bfloat16, jnp.float32
CH = 4
TC = 128
LAST = CH - 1
GELU_K = 0.7978845608028654
GELU_C = 0.044715


def mm(a, b):
    return jnp.dot(a, b, preferred_element_type=F32)


def mm_nt(a, b):
    return lax.dot_general(a, b, (((1,), (1,)), ((), ())), preferred_element_type=F32)


def loop(lo, hi, body, unroll=1):
    def step(i, carry):
        body(i)
        return carry

    lax.fori_loop(lo, hi, step, 0, unroll=unroll)


def aligned(i, size):
    return pl.ds(pl.multiple_of(i * size, size), size)


def low_half():
    return lax.broadcasted_iota(jnp.int32, (1, 8, 128), 1) < 4


def kernel(
    tok_hbm, w_ref, tgt_hbm,
    tg_out, grads_out,
    tok_raw, tgt_raw, tokT, tgtT, stage, stage2, stage3,
    gath, wfull, lw, lwT, rw, rwT,
    gp, fsend, frecv, bsend, brecv, lgrad, rgrad,
    rs0, rs_x, rs2, rs_z,
    in_sem, agz_s, agz_r, agx_s, agx_r, agc_s, agc_r,
    f_s, f_r, b_s, b_r, q_s, q_r, rx_s, rx_r, rz_s, rz_r, qx_s, qx_r, qz_s, qz_r,
):
    dp, mp = lax.axis_index("dp"), lax.axis_index("mp")
    z, x, core = dp // 8, lax.rem(dp // 2, 4), lax.rem(dp, 2)
    hi, y = mp // 4, lax.rem(mp, 4)

    def z_peer(o):
        return (lax.rem(z + o, 4) * 8 + x * 2 + core, mp)

    def xc_of(k):
        return lax.rem(x + lax.rem(k, 4), 4), lax.rem(core + k // 4, 2)

    def xc_peer(k):
        px, pc = xc_of(k)
        return (z * 8 + px * 2 + pc, mp)

    def m_of(k):
        return lax.rem(hi + k // 4, 2) * 4 + lax.rem(y + lax.rem(k, 4), 4)

    def remote(src, dst, ss, rs, dev):
        return pltpu.make_async_remote_copy(
            src_ref=src, dst_ref=dst, send_sem=ss, recv_sem=rs, device_id=dev, device_id_type=MESH
        )

    barrier = pltpu.get_barrier_semaphore()
    peers = [z_peer(o) for o in (1, 2, 3)] + [xc_peer(k) for k in range(1, 8)]
    peers += [(dp, m_of(k)) for k in range(1, 8)]
    for dev in peers:
        pl.semaphore_signal(barrier, inc=1, device_id=dev, device_id_type=MESH)

    def tok_in(c):
        return pltpu.make_async_copy(tok_hbm.at[aligned(c, TC)], tok_raw.at[c], in_sem.at[0, c])

    def tgt_in(c):
        return pltpu.make_async_copy(tgt_hbm.at[aligned(c, TC)], tgt_raw.at[c], in_sem.at[1, c])

    loop(0, CH, lambda c: tok_in(c).start())
    loop(0, CH, lambda c: tgt_in(c).start())
    for f in (0, 1):
        for h in (0, 1):
            gath[f, h, core, x, z] = w_ref[f, h]
    pl.semaphore_wait(barrier, len(peers))

    def ag_z(f, h, o):
        piece = gath.at[f, h, core, x, z]
        return remote(piece, piece, agz_s.at[f, h, o - 1], agz_r.at[f, h, o - 1], z_peer(o))

    def ag_x(f, h, o):
        piece = gath.at[f, h, core, x]
        return remote(piece, piece, agx_s.at[f, h, o - 1], agx_r.at[f, h, o - 1], xc_peer(o))

    def ag_c(f, h, o):
        piece = gath.at[f, h, core, lax.rem(x + 4 - o, 4)]
        return remote(piece, piece, agc_s.at[f, h, o], agc_r.at[f, h, o], xc_peer(4))

    def gather_first(f, h):
        for o in (1, 2, 3):
            ag_z(f, h, o).start()

    def gather_second(f, h):
        for o in (1, 2, 3):
            ag_z(f, h, o).wait_recv()
        for o in (1, 2, 3):
            ag_x(f, h, o).start()
        ag_c(f, h, 0).start()

    def gather_third(f, h):
        for o in (1, 2, 3):
            ag_x(f, h, o).wait_recv()
            ag_c(f, h, o).start()

    def gather_end(f, h):
        for o in (0, 1, 2, 3):
            ag_c(f, h, o).wait_recv()

    def spread(raw, outT, c):
        stage[: TC * 16, :] = raw[c].astype(F32).reshape(TC * 16, 128)

        def one(n):
            rows = stage[pl.ds(n, TC, stride=16), :]
            outT[c, n] = rows.T.astype(BF)

        loop(0, 16, one, 4)

    def tokens_ready(c):
        tok_in(c).wait()
        spread(tok_raw, tokT, c)

    def targets_ready(c):
        tgt_in(c).wait()
        spread(tgt_raw, tgtT, c)

    def assemble(f, h, w, wT):
        def pair(m):
            mx, mz = lax.rem(m, 4), m // 4
            a = gath[f, h, 0, mx, mz].astype(F32).reshape(4, 8, 128)
            b = gath[f, h, 1, mx, mz].astype(F32).reshape(4, 8, 128)
            low = low_half()
            rows = aligned(m, 8)
            wfull[4 * h : 4 * h + 4, 0, rows, :] = jnp.where(low, a, pltpu.roll(b, 4, 1))
            wfull[4 * h : 4 * h + 4, 1, rows, :] = jnp.where(low, pltpu.roll(a, 4, 1), b)

        loop(0, 16, pair, 4)

        def one(n):
            full = wfull[n // 2, lax.rem(n, 2)]
            w[n] = full.astype(BF)
            wT[n] = full.T.astype(BF)

        loop(8 * h, 8 * h + 8, one, 4)

    def fwd_copy(c, k):
        return remote(
            fsend.at[c, m_of(k)], frecv.at[c, mp], f_s.at[c, k - 1], f_r.at[c, k - 1], (dp, m_of(k))
        )

    def bwd_copy(c, k):
        return remote(
            bsend.at[c, m_of(k)], brecv.at[c, mp], b_s.at[c, k - 1], b_r.at[c, k - 1], (dp, m_of(k))
        )

    def quarter_copy(q, k):
        part = pl.ds(4 * q, 4)
        return remote(
            bsend.at[LAST, m_of(k), part], brecv.at[LAST, mp, part],
            q_s.at[q, k - 1], q_r.at[q, k - 1], (dp, m_of(k)),
        )

    def regroup(src, g, m):
        return src[pl.ds(g * 16 + m, 16, stride=128), :].astype(BF)

    def forward_part(c, jh, lo, hi_n):
        rows = aligned(jh, 64)

        def one(n):
            pre = mm(lwT[n, rows, :], tokT[c, n])
            sq = pre * pre
            th = jnp.tanh(pre * (GELU_K + (GELU_K * GELU_C) * sq))
            half = 0.5 + 0.5 * th
            gp[c, n, rows, :] = half + (0.5 * pre) * (1.0 - th * th) * (
                GELU_K + (3.0 * GELU_K * GELU_C) * sq
            )
            stage2[pl.ds(pl.multiple_of(n * 128 + jh * 64, 64), 64), :] = pre * half

        loop(lo, hi_n, one, 4)

    def forward_send(c, lo, hi_k):
        def send(k):
            g = m_of(k)
            for m in range(16):
                fsend[c, g, m] = regroup(stage2, g, m)
            fwd_copy(c, k).start()

        loop(lo, hi_k, send)

    def forward_rest(c):
        forward_part(c, hi, 0, 16)
        forward_send(c, 1, 4)
        for m in range(16):
            frecv[c, mp, m] = regroup(stage2, mp, m)

    for h in (0, 1):
        gather_first(0, h)
    tokens_ready(0)
    for h in (0, 1):
        gather_second(0, h)
    for h in (0, 1):
        gather_first(1, h)
    tokens_ready(1)
    for h in (0, 1):
        gather_third(0, h)
    for h in (0, 1):
        gather_second(1, h)
    for h in (0, 1):
        gather_end(0, h)
        assemble(0, h, lw, lwT)
        forward_part(0, 1 - hi, 8 * h, 8 * h + 8)
    forward_send(0, 4, 8)
    forward_rest(0)

    def forward(c):
        forward_part(c, 1 - hi, 0, 16)
        forward_send(c, 4, 8)
        forward_rest(c)

    forward(1)
    for h in (0, 1):
        gather_third(1, h)

    for h in (0, 1):
        gather_end(1, h)
        assemble(1, h, rw, rwT)

    lgrad[...] = jnp.zeros_like(lgrad)
    rgrad[...] = jnp.zeros_like(rgrad)

    def right(c):
        def one(n):
            act = frecv[c, :, n].reshape(128, TC)
            out = mm(rwT[n], act)
            dout = (out - tgtT[c, n].astype(F32)).astype(BF)
            q, s = n // 2, lax.rem(n, 2)
            rgrad[q, s] = rgrad[q, s] + mm_nt(act, dout)
            stage2[aligned(n, 128), :] = mm(rw[n], dout)

        loop(0, 16, one, 4)
        for m in range(16):
            brecv[c, mp, m] = regroup(stage2, mp, m)

        def fill(k):
            g = m_of(k)
            for m in range(16):
                bsend[c, g, m] = regroup(stage2, g, m)

        loop(1, 8, fill)

    def first(i):
        return lax.rem(i + 3, 7) + 1

    def send_back(c):
        loop(0, 7, lambda i: bwd_copy(c, first(i)).start())

    def sent(copy, u):
        loop(1, 8, lambda k: copy(u, k).wait_send())

    def turn(c):
        targets_ready(c)

        @pl.when(c < 2)
        def _():
            tokens_ready(c + 2)
            sent(fwd_copy, 2 * c)
            forward(c + 2)

        loop(1, 8, lambda k: fwd_copy(c, k).wait_recv())
        right(c)

        @pl.when(c == 0)
        def _():
            sent(fwd_copy, 1)
            send_back(0)

        @pl.when(c == 1)
        def _():
            sent(bwd_copy, 0)
            send_back(1)

        @pl.when(c == 2)
        def _():
            sent(fwd_copy, 3)
            send_back(2)

    loop(0, CH, turn)

    def send_quarter(q):
        loop(0, 7, lambda i: quarter_copy(q, first(i)).start())

    def pieces(f, q, grad):
        def pair(m):
            mx, mz = lax.rem(m, 4), m // 4
            rows = aligned(m, 8)
            a, b = grad[2 * q : 2 * q + 2, 0, rows, :], grad[2 * q : 2 * q + 2, 1, rows, :]
            low = low_half()
            rs0[f, 0, mx, q, mz] = jnp.where(low, a, pltpu.roll(b, 4, 1)).reshape(16, 128).astype(BF)
            rs0[f, 1, mx, q, mz] = jnp.where(low, pltpu.roll(a, 4, 1), b).reshape(16, 128).astype(BF)

        loop(0, 16, pair, 4)

    def add_first(f, q):
        for m in range(4):
            total = rs0[f, core, x, q, m].astype(F32)
            for k in range(7):
                total = total + rs_x[f, k, q, m].astype(F32)
            rs2[f, m, q] = total.astype(BF)

    def add_last(f, q, out):
        total = rs2[f, z, q].astype(F32)
        for o in range(3):
            total = total + rs_z[f, o, q].astype(F32)
        out[16 * q : 16 * q + 16, :] = total

    def rx_copy(k):
        px, pc = xc_of(k)
        return remote(rs0.at[1, pc, px], rs_x.at[1, k - 1], rx_s.at[k - 1], rx_r.at[k - 1], xc_peer(k))

    def rz_copy(o):
        return remote(
            rs2.at[1, lax.rem(z + o, 4)], rs_z.at[1, o - 1], rz_s.at[o - 1], rz_r.at[o - 1], z_peer(o)
        )

    def qx_copy(q, k):
        px, pc = xc_of(k)
        return remote(
            rs0.at[0, pc, px, q], rs_x.at[0, k - 1, q], qx_s.at[q, k - 1], qx_r.at[q, k - 1], xc_peer(k)
        )

    def qz_copy(q, o):
        return remote(
            rs2.at[0, lax.rem(z + o, 4), q], rs_z.at[0, o - 1, q],
            qz_s.at[q, o - 1], qz_r.at[q, o - 1], z_peer(o),
        )

    def left_part(c, lo, hi_n):
        def one(n):
            back = brecv[c, :, n].reshape(128, TC).astype(F32)
            dpre = (back * gp[c, n]).astype(BF)
            q, s = n // 2, lax.rem(n, 2)
            lgrad[q, s] = lgrad[q, s] + mm_nt(tokT[c, n], dpre)
            stage3[pl.ds(n, TC, stride=16), :] = mm(lw[n], dpre).T

        loop(lo, hi_n, one, 4)

    def left_out(c):
        def some(i):
            rows = stage3[aligned(i, 256), :].astype(BF).reshape(16, 16, 128)
            tg_out[pl.ds(c * TC + i * 16, 16)] = rows

        loop(0, 8, some)

    def left(c):
        left_part(c, 0, 16)
        left_out(c)

    for q in range(4):
        pieces(1, q, rgrad)
    loop(1, 8, lambda k: rx_copy(k).start())
    loop(1, 8, lambda k: bwd_copy(0, k).wait_recv())
    left(0)
    sent(bwd_copy, 1)
    send_quarter(0)
    send_quarter(1)
    send_quarter(2)
    loop(1, 8, lambda k: bwd_copy(1, k).wait_recv())
    loop(1, 8, lambda k: rx_copy(k).wait_recv())
    for q in range(4):
        add_first(1, q)
    for o in (1, 2, 3):
        rz_copy(o).start()
    left(1)
    for f in (0, 1):
        for h in (0, 1):
            for o in (1, 2, 3):
                ag_z(f, h, o).wait_send()
                ag_x(f, h, o).wait_send()
            for o in (0, 1, 2, 3):
                ag_c(f, h, o).wait_send()
    loop(1, 8, lambda k: rx_copy(k).wait_send())
    sent(bwd_copy, 2)
    loop(1, 8, lambda k: bwd_copy(2, k).wait_recv())
    left(2)
    for o in (1, 2, 3):
        rz_copy(o).wait()
    for q in range(4):
        add_last(1, q, grads_out.at[1])

    def quarter(q):
        if q == 0:
            sent(quarter_copy, 0)
            send_quarter(3)
        loop(1, 8, lambda k: quarter_copy(q, k).wait_recv())
        left_part(LAST, 4 * q, 4 * q + 4)
        pieces(0, q, lgrad)
        loop(0, 7, lambda i: qx_copy(q, lax.rem(i + 1, 7) + 1).start())

    def second(q):
        loop(1, 8, lambda k: qx_copy(q, k).wait_recv())
        add_first(0, q)
        for o in (1, 2, 3):
            qz_copy(q, o).start()

    for q in range(4):
        quarter(q)
    second(0)
    second(1)
    second(2)
    left_out(LAST)
    loop(1, 4, lambda q: sent(quarter_copy, q))
    loop(0, 3, lambda q: sent(qx_copy, q))
    second(3)
    for q in range(4):
        for o in (1, 2, 3):
            qz_copy(q, o).wait_recv()
        add_last(0, q, grads_out.at[0])

    sent(qx_copy, 3)
    for q in range(4):
        for o in (1, 2, 3):
            qz_copy(q, o).wait_send()


def step(tokens, left_factor, right_factor, target):
    V = pltpu.VMEM
    D = pltpu.SemaphoreType.DMA
    hbm = pl.BlockSpec(memory_space=pltpu.HBM)
    vmem = pl.BlockSpec(memory_space=pltpu.VMEM)
    sq = (128, 128)
    scratch = [
        V((CH, TC, 16, 128), BF), V((CH, TC, 16, 128), BF),
        V((CH, 16, 128, TC), BF), V((CH, 16, 128, TC), BF),
        V((TC * 16 + 16, 128), F32), V((17 * 128, TC), F32), V((TC * 16 + 16, 128), F32),
        V((2, 2, 2, 4, 4, 32, 128), BF), V((8, 2) + sq, F32),
        V((16,) + sq, BF), V((16,) + sq, BF), V((16,) + sq, BF), V((16,) + sq, BF),
        V((CH, 16, 128, TC), F32),
        V((CH, 8, 16, 16, TC), BF), V((CH, 8, 16, 16, TC), BF),
        V((CH, 8, 16, 16, TC), BF), V((CH, 8, 16, 16, TC), BF),
        V((8, 2) + sq, F32), V((8, 2) + sq, F32),
        V((2, 2, 4, 4, 4, 16, 128), BF), V((2, 7, 4, 4, 16, 128), BF),
        V((2, 4, 4, 16, 128), BF), V((2, 3, 4, 16, 128), BF),
        D((2, CH)),
        D((2, 2, 3)), D((2, 2, 3)), D((2, 2, 3)), D((2, 2, 3)), D((2, 2, 4)), D((2, 2, 4)),
        D((CH, 7)), D((CH, 7)), D((CH, 7)), D((CH, 7)), D((4, 7)), D((4, 7)),
        D((7,)), D((7,)), D((3,)), D((3,)), D((4, 7)), D((4, 7)), D((4, 3)), D((4, 3)),
    ]
    which = lax.broadcasted_iota(jnp.int32, (2, 16, 4, 128), 0)
    factors = jnp.where(which == 0, left_factor[None], right_factor[None])
    factors = factors.astype(BF).reshape(2, 2, 32, 128)
    tg, grads = pl.pallas_call(
        kernel,
        name="monarch",
        out_shape=(
            jax.ShapeDtypeStruct((CH * TC, 16, 128), BF),
            jax.ShapeDtypeStruct((2, 64, 128), F32),
        ),
        in_specs=[hbm, vmem, hbm],
        out_specs=(vmem, vmem),
        scratch_shapes=scratch,
        compiler_params=pltpu.CompilerParams(
            collective_id=0, has_side_effects=True, vmem_limit_bytes=51 << 20
        ),
    )(tokens, factors, target)
    lg, rg = grads.reshape(2, 16, 4, 128)
    return tg, lg, rg


def solution(mesh):
    in_specs = (P("dp", "mp", None), P("mp", "dp", None), P("mp", "dp", None), P("dp", "mp", None))
    out_specs = (P("dp", "mp", None), P("mp", "dp", None), P("mp", "dp", None))
    return jax.shard_map(step, mesh=mesh, in_specs=in_specs, out_specs=out_specs, check_vma=False)
```
